512 devices in a mesh: hist: 4 (over y_hi, core), seq: 128 (over z, y_lo, x).
Axes of the slice: x: 4, y: 8 (y_hi: 2, y_lo: 4; y = y_hi * 4 + y_lo), z: 8, core: 2. Of those that a mesh axis runs over, the one named last changes fastest.
Arguments:
- queries: bfloat16 [131072, 1600], P(('hist', 'seq')), parts along dimension 0, may hold values from -6 to 6, as said below
- keys: bfloat16 [131072, 1600], P(('hist', 'seq')), parts along dimension 0, may hold values from -6 to 6, as said below
- values: bfloat16 [131072, 1600], P(('hist', 'seq')), parts along dimension 0, may hold values from -6 to 6
Outputs:
- attended: bfloat16 [131072, 1600], P(('hist', 'seq')), parts along dimension 0
The draws below stay inside these ranges and needn't reach their ends.
There are 4 independent parts, one for each index of `hist`. The reference program is written for one: setup_inputs(seed, part) draws one part's arguments, and reference() takes and returns one part's arrays. A program takes and returns all parts, laid end to end along the dimension named above; each array names one. Nothing has to cross between parts.
Inputs may be any that keep to these rules, and one draw needn't show every extreme that they name: `queries`: entries of the query and key projections. `keys`: entries of the query and key projections.
All inputs are finite; a program needn't handle non-finite values.
Results may differ from the reference program's by a relative error of at most 0.009.
Values may be sent and summed in bfloat16 or wider, within the bound.
No kernel may reach another device: no remote copies, remote signals or barrier semaphores. Data moves between devices by JAX's collectives and lax.ppermute only.
A program may use at most 64 MiB of HBM per device.

```python
import jax
import jax.numpy as jnp
from jax import lax

D = 1600
HEADS = 25
HEAD_DIM = 64
TOK_DEV = 256
WIN = 3
SEQLEN = 32768
N_SEQ = 128


def draw_queries(key, part):
    key = jax.random.fold_in(key, 11)
    out = jnp.clip(jax.random.normal(key, (SEQLEN, D), jnp.float32), -6.0, 6.0)
    return out.astype(jnp.bfloat16)


def draw_keys(key, part):
    key = jax.random.fold_in(key, 23)
    out = jnp.clip(jax.random.normal(key, (SEQLEN, D), jnp.float32), -6.0, 6.0)
    return out.astype(jnp.bfloat16)


def levels(rng, extent, pieces, least, high):
    level, own = 1.0, jax.random.fold_in(rng, 6)
    for axis_at, blocks in pieces:
        steps = jnp.exp(jax.random.uniform(jax.random.fold_in(own, axis_at), (blocks,), jnp.float32, least / len(pieces), high / len(pieces)))
        level = level * jnp.repeat(steps, extent[axis_at] // blocks).reshape([-1 if axis == axis_at else 1 for axis in range(len(extent))])
    return level


def bell_draw(stream_key, extent, spread, limit, pieces=(), kind=jnp.bfloat16):
    level = levels(stream_key, extent, pieces, -0.22, 0.18) if pieces else 1.0
    values = jax.random.normal(stream_key, extent, jnp.float32) * spread * level
    return jnp.minimum(jnp.maximum(values, -limit), limit).astype(kind)


def setup_inputs(seed: int = 0, part: int = 0) -> dict:
    arg_keys = jax.random.split(jax.random.key(seed), 4)
    part_splits = jax.random.split(jax.random.fold_in(arg_keys[3], part), 4)
    return {
        "queries": draw_queries(jax.random.fold_in(jax.random.fold_in(arg_keys[3], part), 71), part),
        "keys": draw_keys(jax.random.fold_in(jax.random.fold_in(arg_keys[3], part), 71), part),
        "values": bell_draw(part_splits[2], (SEQLEN, D), 1.0, 6.0, ((0, 128),)),
    }


def key_block(qblk, kblk, vblk, allowed):
    scale = HEAD_DIM ** -0.5
    score = jnp.einsum("qhd,khd->hqk", qblk.astype(jnp.float32), kblk.astype(jnp.float32), precision=lax.Precision.HIGHEST) * scale
    score = jnp.where(allowed[None], score, -1e30)
    top = jnp.max(score, axis=-1)
    expo = jnp.where(allowed[None], jnp.exp(score - top[..., None]), 0.0)
    total = jnp.sum(expo, axis=-1)
    low_weight = expo.astype(jnp.bfloat16).astype(jnp.float32)
    summed = jnp.einsum("hqk,khd->hqd", low_weight, vblk.astype(jnp.float32), precision=lax.Precision.HIGHEST)
    return top, total, summed


def reference(queries, keys, values):
    pad_rows = WIN * TOK_DEV
    keys_pad = jnp.concatenate([jnp.zeros((pad_rows, D), keys.dtype), keys], axis=0)
    values_pad = jnp.concatenate([jnp.zeros((pad_rows, D), values.dtype), values], axis=0)
    local = jnp.arange(TOK_DEV, dtype=jnp.int32)

    def one_block(block):
        start = (block * TOK_DEV).astype(jnp.int32)
        qblk = lax.dynamic_slice_in_dim(queries, start, TOK_DEV, 0).reshape(TOK_DEV, HEADS, HEAD_DIM)
        parts = []
        for distance in range(WIN + 1):
            offset = (start + (WIN - distance) * TOK_DEV).astype(jnp.int32)
            kblk = lax.dynamic_slice_in_dim(keys_pad, offset, TOK_DEV, 0).reshape(TOK_DEV, HEADS, HEAD_DIM)
            vblk = lax.dynamic_slice_in_dim(values_pad, offset, TOK_DEV, 0).reshape(TOK_DEV, HEADS, HEAD_DIM)
            if distance == 0:
                allowed = local[None, :] <= local[:, None]
            else:
                allowed = jnp.broadcast_to(block >= distance, (TOK_DEV, TOK_DEV))
            parts.append(key_block(qblk, kblk, vblk, allowed))
        row_top = parts[0][0]
        for part_now in parts[1:]:
            row_top = jnp.maximum(row_top, part_now[0])
        total = jnp.zeros_like(row_top)
        summed = jnp.zeros_like(parts[0][2])
        for top, tot, summ in parts:
            factor = jnp.exp(top - row_top)
            total = total + tot * factor
            summed = summed + summ * factor[..., None]
        mixed = summed / total[..., None]
        return jnp.transpose(mixed, (1, 0, 2)).reshape(TOK_DEV, D).astype(jnp.bfloat16)

    blocks = lax.map(one_block, jnp.arange(N_SEQ, dtype=jnp.int32))
    return blocks.reshape(SEQLEN, D)
```

```python
import jax
import jax.numpy as jnp
from jax import lax
from jax.experimental import pallas as pl
from jax.experimental.pallas import tpu as pltpu
from jax.sharding import PartitionSpec as P

HEADS = 25
WIDTH = 64
SPLIT = 13
STAT = 16
SCALE = WIDTH ** -0.5 * 1.4426950408889634
NEG = -1e30
BIG = 1e30


def scores(key_cols, query_cols):
    return lax.dot_general(key_cols, query_cols, (((0,), (0,)), ((), ())), preferred_element_type=jnp.float32)


def attend_kernel(first, heads, flags, q_own, q_mate, k_own, v_own, r1, r3, y1, y3, part, part_lse, msg, s_own, s_mate, mate_lse):
    even, ok_x, ok_z, is0 = [flags[i] > 0 for i in range(4)]
    rows = q_own.shape[1]
    causal = lax.broadcasted_iota(jnp.int32, (rows, rows), 0) <= lax.broadcasted_iota(jnp.int32, (rows, rows), 1)

    def here(h):
        return pl.ds(pl.multiple_of(h * WIDTH, WIDTH), WIDTH)

    def there(h):
        return pl.ds(pl.multiple_of((first + h) * WIDTH, WIDTH), WIDTH)

    def own_scores(h):
        query = q_own[there(h)]
        s_own[:rows] = jnp.where(causal, scores(k_own[there(h)], query), NEG)
        s_own[rows:] = scores(jnp.where(is0, r3[here(h)], r1[here(h)]), query)

    def mate_scores(h):
        query = q_mate[there(h)]
        s_mate[:rows] = scores(jnp.where(even, k_own[there(h)], y1[here(h)]), query)
        s_mate[rows:] = scores(jnp.where(is0, r3[here(h)], r1[here(h)]), query)

    def softmax(s, ok):
        top_z = jnp.max(s[:rows], axis=0, keepdims=True) * SCALE
        if ok is not None:
            top_z = jnp.where(ok, top_z, NEG)
        top_x = jnp.where(ok_x, jnp.max(s[rows:], axis=0, keepdims=True) * SCALE, NEG)
        top = jnp.maximum(top_z, top_x)
        shift_z = top if ok is None else jnp.where(ok, top, BIG)
        expo_z = jnp.exp2(s[:rows] * SCALE - shift_z)
        expo_x = jnp.exp2(s[rows:] * SCALE - jnp.where(ok_x, top, BIG))
        total = jnp.sum(expo_z, axis=0, keepdims=True) + jnp.sum(expo_x, axis=0, keepdims=True)
        total = jnp.maximum(total, 1e-30)
        weight = jnp.concatenate([expo_z.astype(jnp.bfloat16), expo_x.astype(jnp.bfloat16)], axis=0)
        return weight, 1.0 / total, top + jnp.log2(total)

    own_scores(0)

    def one_head(h, carry):
        v_x = jnp.where(is0, y3[here(h)], r3[here(h)])
        mate_scores(h)
        weight, inverse, lse = softmax(s_own, None)
        value = jnp.concatenate([v_own[there(h)], v_x], axis=1)
        part[here(h)] = jnp.dot(value, weight, preferred_element_type=jnp.float32) * inverse
        part_lse[pl.ds(h, 1)] = lse
        own_scores(jnp.minimum(h + 1, heads - 1))
        weight, inverse, lse = softmax(s_mate, ok_z)
        value = jnp.concatenate([jnp.where(even, v_own[there(h)], y3[here(h)]), v_x], axis=1)
        msg[here(h)] = (jnp.dot(value, weight, preferred_element_type=jnp.float32) * inverse).astype(jnp.bfloat16)
        mate_lse[pl.ds(h, 1)] = lse
        return carry

    mate_lse[...] = jnp.zeros(mate_lse.shape, jnp.float32)
    part_lse[...] = jnp.zeros(part_lse.shape, jnp.float32)
    lax.fori_loop(0, heads, one_head, 0)
    stat = mate_lse[...]
    high = stat.astype(jnp.bfloat16).astype(jnp.float32)
    mid = (stat - high).astype(jnp.bfloat16).astype(jnp.float32)
    stat = jnp.concatenate([high, mid, stat - high - mid], axis=0)
    msg[pl.ds(heads * WIDTH, 3 * STAT)] = stat.astype(jnp.bfloat16)


VMEM = pl.BlockSpec(memory_space=pltpu.VMEM)


def attend(flags, q_own, q_mate, k_own, v_own, r1, r3, y1, y3, first):
    rows = q_own.shape[1]
    heads = r1.shape[0] // WIDTH
    return pl.pallas_call(
        lambda *refs: attend_kernel(first, heads, *refs),
        in_specs=[pl.BlockSpec(memory_space=pltpu.SMEM)] + [VMEM] * 8,
        out_specs=[VMEM] * 3,
        out_shape=[
            jax.ShapeDtypeStruct((heads * WIDTH, rows), jnp.float32),
            jax.ShapeDtypeStruct((STAT, rows), jnp.float32),
            jax.ShapeDtypeStruct((heads * WIDTH + 3 * STAT, rows), jnp.bfloat16),
        ],
        scratch_shapes=[
            pltpu.VMEM((2 * rows, rows), jnp.float32),
            pltpu.VMEM((2 * rows, rows), jnp.float32),
            pltpu.VMEM((STAT, rows), jnp.float32),
        ],
        compiler_params=pltpu.CompilerParams(vmem_limit_bytes=24 * 2**20),
        cost_estimate=pl.CostEstimate(
            flops=heads * 4 * 4 * rows * rows * WIDTH,
            bytes_accessed=heads * WIDTH * rows * 24,
            transcendentals=heads * 4 * rows * rows,
        ),
        name="attend",
    )(flags, q_own, q_mate, k_own, v_own, r1, r3, y1, y3)


def merge_kernel(heads, part, part_lse, msg, *rest):
    out = rest[-1]
    at = 0
    if len(rest) > 1:
        at = rest[0].shape[0]
        out[:at] = rest[0][...]
    stat = msg[pl.ds(heads * WIDTH, 3 * STAT)].astype(jnp.float32)
    gap = stat[:STAT] + stat[STAT : 2 * STAT] + stat[2 * STAT :] - part_lse[...]
    mine, theirs = 1.0 / (1.0 + jnp.exp2(gap)), 1.0 / (1.0 + jnp.exp2(-gap))
    for h in range(heads):
        src = pl.ds(h * WIDTH, WIDTH)
        both = part[src] * mine[h : h + 1] + msg[src].astype(jnp.float32) * theirs[h : h + 1]
        out[pl.ds(at + h * WIDTH, WIDTH)] = both.astype(jnp.bfloat16)


def merge(part, part_lse, msg, *before):
    size, rows = part.shape
    done = sum(b.shape[0] for b in before)
    return pl.pallas_call(
        lambda *refs: merge_kernel(size // WIDTH, *refs),
        in_specs=[VMEM] * (3 + len(before)),
        out_specs=VMEM,
        out_shape=jax.ShapeDtypeStruct((done + size, rows), jnp.bfloat16),
        compiler_params=pltpu.CompilerParams(vmem_limit_bytes=24 * 2**20),
        cost_estimate=pl.CostEstimate(flops=size * rows * 4, bytes_accessed=size * rows * 8, transcendentals=0),
        name="merge",
    )(part, part_lse, msg, *before)


def shards(queries, keys, values):
    length = lax.axis_size("seq")
    position = lax.axis_index("seq")
    column = position % 4
    even = column % 2 == 0
    q, k, v = queries.T, keys.T, values.T
    cut = SPLIT * WIDTH
    k1, k2, v1, v2 = k[:cut], k[cut:], v[:cut], v[cut:]
    swap = [(i, i ^ 1) for i in range(length)]
    to_x = [(i, i + (3, 1, 3, -3)[i % 4]) for i in range(length)]
    to_x = [(i, j) for i, j in to_x if j < length]
    to_y = [(i, i + 4) for i in range(length - 4) if i % 2]
    to_y0 = [(i, i + 4) for i in range(length - 4) if i % 4 != 2]

    def send_x(most, from3):
        return lax.ppermute(jnp.where(column == 3, from3, most), "seq", to_x)

    def send_y0(most, from0):
        return lax.ppermute(jnp.where(column == 0, from0, most), "seq", to_y0)

    r1, y1 = send_x(k1, v1), lax.ppermute(k1, "seq", to_y)
    q_mate = lax.ppermute(q, "seq", swap)
    r2, y2 = send_x(k2, v2), lax.ppermute(k2, "seq", to_y)
    r3, y3 = send_x(v1, y1), send_y0(v1, r1)
    r4, y4 = send_x(v2, y2), send_y0(v2, r2)
    ok_x = jnp.where(even, position >= 1, position >= 3)
    ok_z = jnp.where(even, position >= 0, position >= 4)
    flags = jnp.stack([even, ok_x, ok_z, column == 0]).astype(jnp.int32)
    part1, lse1, msg1 = attend(flags, q, q_mate, k, v, r1, r3, y1, y3, 0)
    flags, msg1 = lax.optimization_barrier((flags, msg1))
    msg1 = lax.ppermute(msg1, "seq", swap)
    part2, lse2, msg2 = attend(flags, q, q_mate, k, v, r2, r4, y2, y4, SPLIT)
    msg2 = lax.ppermute(msg2, "seq", swap)
    return merge(part2, lse2, msg2, merge(part1, lse1, msg1)).T


def solution(mesh):
    return jax.shard_map(
        shards,
        mesh=mesh,
        in_specs=(P(("hist", "seq"), None), P(("hist", "seq"), None), P(("hist", "seq"), None)),
        out_specs=P(("hist", "seq"), None),
        check_vma=False,
    )
```

```python
import jax
import jax.numpy as jnp
from jax import lax
from jax.experimental import pallas as pl
from jax.experimental.pallas import tpu as pltpu
from jax.sharding import PartitionSpec as P

HEADS = 25
WIDTH = 64
GROUP = 5
CHUNKS = (3, 2)
STEP = GROUP * WIDTH
ONES = 16
STAT = 16
MSG = STEP + STAT
SCALE = WIDTH ** -0.5 * 1.4426950408889634
NEG = -1e30


def scores(key_cols, query_cols):
    return lax.dot_general(key_cols, query_cols, (((0,), (0,)), ((), ())), preferred_element_type=jnp.float32)


def fold_max(tile):
    return jnp.max(tile.reshape(tile.shape[0] // 8, 8, tile.shape[1]), axis=0)


def top_of(folded):
    return jnp.max(folded, axis=0, keepdims=True) * SCALE


def with_ones(value):
    return jnp.concatenate([value, jnp.ones((ONES, value.shape[1]), value.dtype)], axis=0)


def weights(score, top):
    return jnp.exp2(score * SCALE - top).astype(jnp.bfloat16)


def pipelined(units):
    results, depth = [[] for _ in units], len(units[0])
    for i in range(len(units) + depth - 1):
        for stage in range(depth):
            if 0 <= i - stage < len(units):
                done = results[i - stage]
                done.append(units[i - stage][stage](*done))
    return results


def stack_rows(rows, size):
    fill = [jnp.zeros_like(rows[0])] * (size - len(rows))
    return jnp.concatenate(list(rows) + fill, axis=0)


def diag_kernel(q_any, k_any, v_any, query, key, value, acc, stats, sems):
    rows = query.shape[1]
    half = rows // 2
    later = lax.broadcasted_iota(jnp.int32, (half, half), 0) > lax.broadcasted_iota(jnp.int32, (half, half), 1)

    def copies(i):
        at = pl.ds(pl.multiple_of(i * STEP, STEP), STEP)
        pairs = (q_any, query), (k_any, key), (v_any, value)
        return [pltpu.make_async_copy(src.at[at], dst.at[at], sems.at[i, j]) for j, (src, dst) in enumerate(pairs)]

    for i in range(HEADS // GROUP):
        for copy in copies(i):
            copy.start()

    def one_group(i, carry):
        for copy in copies(i):
            copy.wait()
        diag_group(i, query, key, value, acc, stats, later)
        return carry

    lax.fori_loop(0, HEADS // GROUP, one_group, 0)


def diag_group(i, query, key, value, acc, stats, later):
    half = later.shape[0]

    def there(g):
        return pl.ds(pl.multiple_of(i * STEP + g * WIDTH, WIDTH), WIDTH)

    def unit(g):
        at = there(g)

        def score():
            q, k = query[at], key[at]
            return scores(k[:, :half], q), scores(k[:, half:], q[:, half:])

        def top(score):
            first, last = score
            corner, last = jnp.where(later, NEG, first[:, :half]), jnp.where(later, NEG, last)
            right = first[:, half:]
            top_a, top_b = top_of(fold_max(corner)), top_of(jnp.maximum(fold_max(right), fold_max(last)))
            return corner, right, last, top_a, top_b

        def weight(score, top):
            corner, right, last, top_a, top_b = top
            upper = jnp.concatenate([weights(corner, top_a), weights(right, top_b)], axis=1)
            lower = jnp.concatenate([jnp.zeros((half, half), jnp.bfloat16), weights(last, top_b)], axis=1)
            return jnp.concatenate([upper, lower], axis=0)

        def product(score, top, weight):
            return jnp.dot(with_ones(value[at]), weight, preferred_element_type=jnp.float32)

        return score, top, weight, product

    done = pipelined([unit(g) for g in range(GROUP)])
    for g in range(GROUP):
        acc[there(g)] = done[g][3][:WIDTH]
    totals = [d[3][WIDTH : WIDTH + 1] for d in done]
    tops = [jnp.concatenate(d[1][3:], axis=1) for d in done]
    stats[i] = jnp.concatenate([stack_rows(tops, 8), stack_rows(totals, 8)], axis=0)


def mix(a, b):
    (acc_a, total_a, top_a), (acc_b, total_b, top_b) = a, b
    top = jnp.maximum(top_a, top_b)
    factor_a, factor_b = jnp.exp2(top_a - top), jnp.exp2(top_b - top)
    total = total_a * factor_a + total_b * factor_b
    return acc_a * (factor_a / total) + acc_b * (factor_b / total), top + jnp.log2(total)


def attend_kernel(first, flags, q_own, k_own, v_own, acc_d, stats_d, q_mate, r1, r3, y1, y3, part, part_lse, msg):
    even, ok_x, ok_z, is0 = [flags[i] > 0 for i in range(4)]
    rows = q_own.shape[1]

    def one_group(i, carry):
        def here(g):
            return pl.ds(pl.multiple_of(i * STEP + g * WIDTH, WIDTH), WIDTH)

        def there(g):
            return pl.ds(pl.multiple_of((first + i) * STEP + g * WIDTH, WIDTH), WIDTH)

        def unit(score, value, ok):
            def top(s):
                return top_of(fold_max(s))

            def weight(s, top):
                return weights(s, top)

            def product(s, top, weight):
                acc = jnp.dot(with_ones(value()), weight, preferred_element_type=jnp.float32)
                return acc[:WIDTH], acc[WIDTH : WIDTH + 1], jnp.where(ok, top, NEG)

            return score, top, weight, product

        def unit_x(g):
            def score():
                key = jnp.where(is0, r3[here(g)], r1[here(g)])
                return scores(key, jnp.concatenate([q_own[there(g)], q_mate[there(g)]], axis=1))

            return unit(score, lambda: jnp.where(is0, y3[here(g)], r3[here(g)]), ok_x)

        def unit_z(g):
            def score():
                return scores(jnp.where(even, k_own[there(g)], y1[here(g)]), q_mate[there(g)])

            return unit(score, lambda: jnp.where(even, v_own[there(g)], y3[here(g)]), ok_z)

        done = pipelined([u(g) for g in range(GROUP) for u in (unit_x, unit_z)])
        stats = stats_d[first + i]
        own, mate = [], []
        for g in range(GROUP):
            x, z = done[2 * g][3], done[2 * g + 1][3]
            d = acc_d[there(g)], stats[8 + g : 9 + g], stats[g : g + 1]
            own.append(mix(d, [e[:, :rows] for e in x]))
            mate.append(mix(z, [e[:, rows:] for e in x]))
        for g in range(GROUP):
            part[here(g)] = own[g][0]
            msg[pl.ds(pl.multiple_of(i * MSG + g * WIDTH, 16), WIDTH)] = mate[g][0].astype(jnp.bfloat16)
        part_lse[i] = stack_rows([lse for _, lse in own], 8)
        stat = jnp.concatenate([lse for _, lse in mate], axis=0)
        high = stat.astype(jnp.bfloat16).astype(jnp.float32)
        mid = (stat - high).astype(jnp.bfloat16).astype(jnp.float32)
        stat = stack_rows([high, mid, stat - high - mid, jnp.zeros((1, rows), jnp.float32)], 4)
        msg[pl.ds(pl.multiple_of(i * MSG + STEP, 16), STAT)] = stat.astype(jnp.bfloat16)
        return carry

    lax.fori_loop(0, part_lse.shape[0], one_group, 0)


VMEM = pl.BlockSpec(memory_space=pltpu.VMEM)
ANY = pl.BlockSpec(memory_space=pl.ANY)


def diag(q, k, v):
    size, rows = q.shape
    groups = HEADS // GROUP
    return pl.pallas_call(
        diag_kernel,
        in_specs=[ANY] * 3,
        out_specs=[VMEM] * 5,
        out_shape=[
            *[jax.ShapeDtypeStruct((size, rows), jnp.bfloat16)] * 3,
            jax.ShapeDtypeStruct((size, rows), jnp.float32),
            jax.ShapeDtypeStruct((groups, 16, rows), jnp.float32),
        ],
        scratch_shapes=[pltpu.SemaphoreType.DMA((groups, 3))],
        compiler_params=pltpu.CompilerParams(vmem_limit_bytes=24 * 2**20),
        cost_estimate=pl.CostEstimate(
            flops=HEADS * 4 * rows * rows * WIDTH, bytes_accessed=size * rows * 10, transcendentals=HEADS * rows * rows
        ),
        name="diag",
    )(q, k, v)


def attend(flags, diagonal, q_mate, r1, r3, y1, y3, first):
    size, rows = r1.shape
    heads, groups = size // WIDTH, size // STEP
    return pl.pallas_call(
        lambda *refs: attend_kernel(first, *refs),
        in_specs=[pl.BlockSpec(memory_space=pltpu.SMEM)] + [VMEM] * 10,
        out_specs=[VMEM] * 3,
        out_shape=[
            jax.ShapeDtypeStruct((size, rows), jnp.float32),
            jax.ShapeDtypeStruct((groups, 8, rows), jnp.float32),
            jax.ShapeDtypeStruct((groups * MSG, rows), jnp.bfloat16),
        ],
        compiler_params=pltpu.CompilerParams(vmem_limit_bytes=24 * 2**20),
        cost_estimate=pl.CostEstimate(
            flops=heads * 3 * 4 * rows * rows * WIDTH,
            bytes_accessed=heads * WIDTH * rows * 24,
            transcendentals=heads * 3 * rows * rows,
        ),
        name="attend",
    )(flags, *diagonal, q_mate, r1, r3, y1, y3)


def merge_kernel(part, part_lse, msg, *rest):
    out = rest[-1]
    at = 0
    if len(rest) > 1:
        at = rest[0].shape[0]
        out[:at] = rest[0][...]
    for i in range(part_lse.shape[0]):
        stat = msg[pl.ds(i * MSG + STEP, STAT)].astype(jnp.float32)
        lse = stat[:GROUP] + stat[GROUP : 2 * GROUP] + stat[2 * GROUP : 3 * GROUP]
        gap = lse - part_lse[i, :GROUP]
        mine, theirs = 1.0 / (1.0 + jnp.exp2(gap)), 1.0 / (1.0 + jnp.exp2(-gap))
        for g in range(GROUP):
            row, src = i * STEP + g * WIDTH, pl.ds(i * MSG + g * WIDTH, WIDTH)
            both = part[pl.ds(row, WIDTH)] * mine[g : g + 1] + msg[src].astype(jnp.float32) * theirs[g : g + 1]
            out[pl.ds(at + row, WIDTH)] = both.astype(jnp.bfloat16)


def merge(part, part_lse, msg, *before):
    size, rows = part.shape
    done = sum(b.shape[0] for b in before)
    return pl.pallas_call(
        merge_kernel,
        in_specs=[VMEM] * (3 + len(before)),
        out_specs=VMEM,
        out_shape=jax.ShapeDtypeStruct((done + size, rows), jnp.bfloat16),
        compiler_params=pltpu.CompilerParams(vmem_limit_bytes=24 * 2**20),
        cost_estimate=pl.CostEstimate(flops=size * rows * 4, bytes_accessed=size * rows * 8, transcendentals=0),
        name="merge",
    )(part, part_lse, msg, *before)


def shards(queries, keys, values):
    length = lax.axis_size("seq")
    position = lax.axis_index("seq")
    column = position % 4
    even = column % 2 == 0
    q, k, v = queries.T, keys.T, values.T
    swap = [(i, i ^ 1) for i in range(length)]
    to_x = [(i, i + (3, 1, 3, -3)[i % 4]) for i in range(length)]
    to_x = [(i, j) for i, j in to_x if j < length]
    to_y = [(i, i + 4) for i in range(length - 4) if i % 2]
    to_y0 = [(i, i + 4) for i in range(length - 4) if i % 4 != 2]

    cut = CHUNKS[0] * STEP
    y_1, y_2 = k[:cut], k[cut:]
    x_1, x_2 = jnp.where(column == 3, v[:cut], y_1), jnp.where(column == 3, v[cut:], y_2)
    r1, y1 = lax.ppermute(x_1, "seq", to_x), lax.ppermute(y_1, "seq", to_y)
    r2, y2 = lax.ppermute(x_2, "seq", to_x), lax.ppermute(y_2, "seq", to_y)
    q_mate = lax.ppermute(q, "seq", swap)
    r1, y1, *diagonal = lax.optimization_barrier((r1, y1, *diag(q, k, v)))
    value = diagonal[2]

    def send_on(r, y, at):
        return jnp.where(column == 3, y, value[at]), jnp.where(column == 0, r, value[at])

    to_send = send_on(r1, y1, slice(0, cut))
    r3, y3 = lax.ppermute(to_send[0], "seq", to_x), lax.ppermute(to_send[1], "seq", to_y0)
    r2, y2 = lax.optimization_barrier((r2, y2, *to_send))[:2]
    to_send = send_on(r2, y2, slice(cut, None))
    r4, y4 = lax.ppermute(to_send[0], "seq", to_x), lax.ppermute(to_send[1], "seq", to_y0)
    ok_x = jnp.where(even, position >= 1, position >= 3)
    ok_z = jnp.where(even, position >= 0, position >= 4)
    flags = jnp.stack([even, ok_x, ok_z, column == 0]).astype(jnp.int32)
    part1, lse1, msg1 = attend(flags, diagonal, q_mate, r1, r3, y1, y3, 0)
    flags, msg1 = lax.optimization_barrier((flags, msg1))
    msg1 = lax.ppermute(msg1, "seq", swap)
    part2, lse2, msg2 = attend(flags, diagonal, q_mate, r2, r4, y2, y4, CHUNKS[0])
    msg2 = lax.ppermute(msg2, "seq", swap)
    return merge(part2, lse2, msg2, merge(part1, lse1, msg1)).T


def solution(mesh):
    return jax.shard_map(
        shards,
        mesh=mesh,
        in_specs=(P(("hist", "seq"), None), P(("hist", "seq"), None), P(("hist", "seq"), None)),
        out_specs=P(("hist", "seq"), None),
        check_vma=False,
    )
```

```python
import jax
import jax.numpy as jnp
from jax import lax
from jax.experimental import pallas as pl
from jax.experimental.pallas import tpu as pltpu
from jax.sharding import PartitionSpec as P

HEADS = 25
WIDTH = 64
GROUP = 5
HALVES = (2, 3)
CHUNKS = (2, 2, 1)
STEP = GROUP * WIDTH
ONES = 16
STAT = 16
MSG = STEP + STAT
SCALE = WIDTH ** -0.5 * 1.4426950408889634
NEG = -1e30


def scores(key_cols, query_cols):
    return lax.dot_general(key_cols, query_cols, (((0,), (0,)), ((), ())), preferred_element_type=jnp.float32)


def fold_max(tile):
    return jnp.max(tile.reshape(tile.shape[0] // 8, 8, tile.shape[1]), axis=0)


def top_of(folded):
    return jnp.max(folded, axis=0, keepdims=True) * SCALE


def with_ones(value):
    return jnp.concatenate([value, jnp.ones((ONES, value.shape[1]), value.dtype)], axis=0)


def weights(score, top):
    return jnp.exp2(score * SCALE - top).astype(jnp.bfloat16)


def pipelined(units):
    results, depth = [[] for _ in units], len(units[0])
    for i in range(len(units) + depth - 1):
        for stage in range(depth):
            if 0 <= i - stage < len(units):
                done = results[i - stage]
                done.append(units[i - stage][stage](*done))
    return results


def stack_rows(rows, size):
    fill = [jnp.zeros_like(rows[0])] * (size - len(rows))
    return jnp.concatenate(list(rows) + fill, axis=0)


def mix(a, b):
    (acc_a, total_a, top_a), (acc_b, total_b, top_b) = a, b
    top = jnp.maximum(top_a, top_b)
    factor_a, factor_b = jnp.exp2(top_a - top), jnp.exp2(top_b - top)
    total = total_a * factor_a + total_b * factor_b
    return acc_a * (factor_a / total) + acc_b * (factor_b / total), top + jnp.log2(total)


def attend_kernel(first, skip, q_own, q_mate, k_own, v_own, r1, r3, y1, y3, part, part_lse, msg):
    position = lax.axis_index("seq")
    even, is0 = position % 2 == 0, position % 4 == 0
    ok_x, ok_z = (position >= 3) | (even & (position >= 1)), even | (position >= 4)
    rows = q_own.shape[1]
    half = rows // 2
    later = lax.broadcasted_iota(jnp.int32, (half, half), 0) > lax.broadcasted_iota(jnp.int32, (half, half), 1)

    def one_group(i, carry):
        def rows_at(group, g, step=STEP):
            return pl.ds(pl.multiple_of(group * step + g * WIDTH, 16), WIDTH)

        def here(g):
            return rows_at(skip + i, g)

        def there(g):
            return rows_at(first + i, g)

        def unit(score, value, ok):
            def top(s):
                return top_of(fold_max(s))

            def weight(s, top):
                return weights(s, top)

            def product(s, top, weight):
                acc = jnp.dot(with_ones(value()), weight, preferred_element_type=jnp.float32)
                return acc[:WIDTH], acc[WIDTH : WIDTH + 1], jnp.where(ok, top, NEG)

            return score, top, weight, product

        def unit_x(g):
            def score():
                key = jnp.where(is0, y3[here(g)], r1[there(g)])
                return scores(key, jnp.concatenate([q_own[there(g)], q_mate[there(g)]], axis=1))

            return unit(score, lambda: r3[here(g)], ok_x)

        def unit_z(g):
            def score():
                return scores(jnp.where(even, k_own[there(g)], y3[here(g)]), q_mate[there(g)])

            return unit(score, lambda: jnp.where(even, v_own[there(g)], y1[here(g)]), ok_z)

        def unit_d(g):
            def score():
                q, k = q_own[there(g)], k_own[there(g)]
                return scores(k[:, :half], q), scores(k[:, half:], q[:, half:])

            def top(score):
                first, last = score
                corner, last = jnp.where(later, NEG, first[:, :half]), jnp.where(later, NEG, last)
                right = first[:, half:]
                top_a, top_b = top_of(fold_max(corner)), top_of(jnp.maximum(fold_max(right), fold_max(last)))
                return corner, right, last, top_a, top_b

            def weight(score, top):
                corner, right, last, top_a, top_b = top
                upper = jnp.concatenate([weights(corner, top_a), weights(right, top_b)], axis=1)
                lower = jnp.concatenate([jnp.zeros((half, half), jnp.bfloat16), weights(last, top_b)], axis=1)
                return jnp.concatenate([upper, lower], axis=0)

            def product(score, top, weight):
                acc = jnp.dot(with_ones(v_own[there(g)]), weight, preferred_element_type=jnp.float32)
                return acc[:WIDTH], acc[WIDTH : WIDTH + 1], jnp.concatenate(top[3:], axis=1)

            return score, top, weight, product

        done = pipelined([u(g) for g in range(GROUP) for u in (unit_x, unit_z, unit_d)])
        own, mate = [], []
        for g in range(GROUP):
            x, z, d = [done[3 * g + j][3] for j in range(3)]
            own.append(mix(d, [e[:, :rows] for e in x]))
            mate.append(mix(z, [e[:, rows:] for e in x]))
        for g in range(GROUP):
            part[rows_at(i, g)] = own[g][0]
            msg[rows_at(i, g, MSG)] = mate[g][0].astype(jnp.bfloat16)
        part_lse[i] = stack_rows([lse for _, lse in own], 8)
        stat = jnp.concatenate([lse for _, lse in mate], axis=0)
        high = stat.astype(jnp.bfloat16).astype(jnp.float32)
        mid = (stat - high).astype(jnp.bfloat16).astype(jnp.float32)
        stat = stack_rows([high, mid, stat - high - mid, jnp.zeros((1, rows), jnp.float32)], 4)
        msg[pl.ds(pl.multiple_of(i * MSG + STEP, 16), STAT)] = stat.astype(jnp.bfloat16)
        return carry

    lax.fori_loop(0, part_lse.shape[0], one_group, 0)


VMEM = pl.BlockSpec(memory_space=pltpu.VMEM)


def attend(arguments, q_mate, came, first, skip, groups):
    rows = q_mate.shape[1]
    size, heads = groups * STEP, groups * GROUP
    q, k, v = arguments
    return pl.pallas_call(
        lambda *refs: attend_kernel(first, skip, *refs),
        in_specs=[VMEM] * 8,
        out_specs=[VMEM] * 3,
        out_shape=[
            jax.ShapeDtypeStruct((size, rows), jnp.float32),
            jax.ShapeDtypeStruct((groups, 8, rows), jnp.float32),
            jax.ShapeDtypeStruct((groups * MSG, rows), jnp.bfloat16),
        ],
        compiler_params=pltpu.CompilerParams(vmem_limit_bytes=12 * 2**20),
        cost_estimate=pl.CostEstimate(
            flops=heads * 4 * 4 * 4 * rows * rows * WIDTH,
            bytes_accessed=heads * WIDTH * rows * 24,
            transcendentals=heads * 4 * rows * rows,
        ),
        name="attend",
    )(q, q_mate, k, v, *came)


def merge_kernel(part, part_lse, msg, *rest):
    out = rest[-1]
    at = 0
    for before in rest[:-1]:
        out[pl.ds(at, before.shape[0])] = before[...]
        at += before.shape[0]
    for i in range(part_lse.shape[0]):
        stat = msg[pl.ds(i * MSG + STEP, STAT)].astype(jnp.float32)
        lse = stat[:GROUP] + stat[GROUP : 2 * GROUP] + stat[2 * GROUP : 3 * GROUP]
        gap = lse - part_lse[i, :GROUP]
        mine, theirs = 1.0 / (1.0 + jnp.exp2(gap)), 1.0 / (1.0 + jnp.exp2(-gap))
        for g in range(GROUP):
            row, src = i * STEP + g * WIDTH, pl.ds(i * MSG + g * WIDTH, WIDTH)
            both = part[pl.ds(row, WIDTH)] * mine[g : g + 1] + msg[src].astype(jnp.float32) * theirs[g : g + 1]
            out[pl.ds(at + row, WIDTH)] = both.astype(jnp.bfloat16)


def merge(part, part_lse, msg, *before):
    size, rows = part.shape
    done = sum(b.shape[0] for b in before)
    return pl.pallas_call(
        merge_kernel,
        in_specs=[VMEM] * (3 + len(before)),
        out_specs=VMEM,
        out_shape=jax.ShapeDtypeStruct((done + size, rows), jnp.bfloat16),
        compiler_params=pltpu.CompilerParams(vmem_limit_bytes=12 * 2**20),
        cost_estimate=pl.CostEstimate(flops=size * rows * 4, bytes_accessed=size * rows * 8, transcendentals=0),
        name="merge",
    )(part, part_lse, msg, *before)


def shards(queries, keys, values):
    length = lax.axis_size("seq")
    position = lax.axis_index("seq")
    column = position % 4
    q, k, v = queries.T, keys.T, values.T
    swap = [(i, i ^ 1) for i in range(length)]
    to_x = [(i, i + (3, 1, 3, -3)[i % 4]) for i in range(length)]
    to_x = [(i, j) for i, j in to_x if j < length]
    to_y = [(i, i + 4) for i in range(length - 4) if i % 2]
    to_y0 = [(i, i + 4) for i in range(length - 4) if i % 4 != 2]

    cut = HALVES[0] * STEP
    k1, k2, v1, v2 = k[:cut], k[cut:], v[:cut], v[cut:]
    r1 = lax.ppermute(k, "seq", to_x)
    y1, y2 = lax.ppermute(v1, "seq", to_y), lax.ppermute(v2, "seq", to_y)
    q_mate = lax.ppermute(q, "seq", swap)
    send = jnp.where(column == 3, y1, v1)
    r3 = lax.ppermute(send, "seq", to_x)
    r1 = lax.optimization_barrier((r1, send))[0]
    send = jnp.where(column == 0, r1[:cut], k1)
    y3 = lax.ppermute(send, "seq", to_y0)
    r1, y2 = lax.optimization_barrier((r1, y2, send))[:2]
    send = jnp.where(column == 0, r1[cut:], k2)
    y4 = lax.ppermute(send, "seq", to_y0)
    r4 = lax.ppermute(jnp.where(column == 3, y2, v2), "seq", to_x)
    halves, arguments = ((r1, r3, y1, y3), (r1, r4, y2, y4)), (q, k, v)
    results, first = [], 0
    for groups in CHUNKS:
        half = int(first >= HALVES[0])
        part, lse, msg = attend(arguments, q_mate, halves[half], first, first - half * HALVES[0], groups)
        q_mate, msg = lax.optimization_barrier((q_mate, msg))
        results.append((part, lse, lax.ppermute(msg, "seq", swap)))
        first += groups
    before = [merge(*result) for result in results[:-1]]
    return merge(*results[-1], *before).T


def solution(mesh):
    return jax.shard_map(
        shards,
        mesh=mesh,
        in_specs=(P(("hist", "seq"), None), P(("hist", "seq"), None), P(("hist", "seq"), None)),
        out_specs=P(("hist", "seq"), None),
        check_vma=False,
    )
```

```python
import jax
import jax.numpy as jnp
from jax import lax
from jax.experimental import pallas as pl
from jax.experimental.pallas import tpu as pltpu
from jax.sharding import PartitionSpec as P

HEADS = 25
WIDTH = 64
GROUP = 5
HALVES = (2, 3)
CHUNKS = (2, 2, 1)
STEP = GROUP * WIDTH
ONES = 16
STAT = 16
MSG = STEP + STAT
SCALE = WIDTH ** -0.5 * 1.4426950408889634
NEG = -1e30


def scores(key_cols, query_cols):
    return lax.dot_general(key_cols, query_cols, (((0,), (0,)), ((), ())), preferred_element_type=jnp.float32)


def fold_max(tile):
    return jnp.max(tile.reshape(tile.shape[0] // 8, 8, tile.shape[1]), axis=0)


def top_of(folded):
    return jnp.max(folded, axis=0, keepdims=True) * SCALE


def with_ones(value):
    return jnp.concatenate([value, jnp.ones((ONES, value.shape[1]), value.dtype)], axis=0)


def weights(score, top):
    return jnp.exp2(score * SCALE - top).astype(jnp.bfloat16)


def pipelined(units):
    results, depth = [[] for _ in units], len(units[0])
    for i in range(len(units) + depth - 1):
        for stage in range(depth):
            if 0 <= i - stage < len(units):
                done = results[i - stage]
                done.append(units[i - stage][stage](*done))
    return results


def stack_rows(rows, size):
    fill = [jnp.zeros_like(rows[0])] * (size - len(rows))
    return jnp.concatenate(list(rows) + fill, axis=0)


def mix(a, b):
    (acc_a, total_a, top_a), (acc_b, total_b, top_b) = a, b
    top = jnp.maximum(top_a, top_b)
    factor_a, factor_b = jnp.exp2(top_a - top), jnp.exp2(top_b - top)
    total = total_a * factor_a + total_b * factor_b
    return acc_a * (factor_a / total) + acc_b * (factor_b / total), top + jnp.log2(total)


def attend_kernel(first, skip, q_any, qm_any, k_own, v_own, r1, r3, y1, y3, part, part_lse, msg, q_own, q_mate, sems):
    position = lax.axis_index("seq")
    even, is0 = position % 2 == 0, position % 4 == 0
    ok_x, ok_z = (position >= 3) | (even & (position >= 1)), even | (position >= 4)
    rows = q_own.shape[1]
    half = rows // 2
    later = lax.broadcasted_iota(jnp.int32, (half, half), 0) > lax.broadcasted_iota(jnp.int32, (half, half), 1)

    def copies(i):
        src = pl.ds(pl.multiple_of((first + i) * STEP, STEP), STEP)
        dst = pl.ds(pl.multiple_of(i * STEP, STEP), STEP)
        pairs = (q_any, q_own), (qm_any, q_mate)
        return [pltpu.make_async_copy(a.at[src], b.at[dst], sems.at[i, j]) for j, (a, b) in enumerate(pairs)]

    for i in range(part_lse.shape[0]):
        for copy in copies(i):
            copy.start()

    def one_group(i, carry):
        for copy in copies(i):
            copy.wait()

        def rows_at(group, g, step=STEP):
            return pl.ds(pl.multiple_of(group * step + g * WIDTH, 16), WIDTH)

        def here(g):
            return rows_at(skip + i, g)

        def there(g):
            return rows_at(first + i, g)

        def unit(score, value, ok):
            def top(s):
                return top_of(fold_max(s))

            def weight(s, top):
                return weights(s, top)

            def product(s, top, weight):
                acc = jnp.dot(with_ones(value()), weight, preferred_element_type=jnp.float32)
                return acc[:WIDTH], acc[WIDTH : WIDTH + 1], jnp.where(ok, top, NEG)

            return score, top, weight, product

        def unit_x(g):
            def score():
                key = jnp.where(is0, y3[here(g)], r1[there(g)])
                return scores(key, jnp.concatenate([q_own[rows_at(i, g)], q_mate[rows_at(i, g)]], axis=1))

            return unit(score, lambda: r3[here(g)], ok_x)

        def unit_z(g):
            def score():
                return scores(jnp.where(even, k_own[there(g)], y3[here(g)]), q_mate[rows_at(i, g)])

            return unit(score, lambda: jnp.where(even, v_own[there(g)], y1[here(g)]), ok_z)

        def unit_d(g):
            def score():
                q, k = q_own[rows_at(i, g)], k_own[there(g)]
                return scores(k[:, :half], q), scores(k[:, half:], q[:, half:])

            def top(score):
                first, last = score
                corner, last = jnp.where(later, NEG, first[:, :half]), jnp.where(later, NEG, last)
                right = first[:, half:]
                top_a, top_b = top_of(fold_max(corner)), top_of(jnp.maximum(fold_max(right), fold_max(last)))
                return corner, right, last, top_a, top_b

            def weight(score, top):
                corner, right, last, top_a, top_b = top
                upper = jnp.concatenate([weights(corner, top_a), weights(right, top_b)], axis=1)
                lower = jnp.concatenate([jnp.zeros((half, half), jnp.bfloat16), weights(last, top_b)], axis=1)
                return jnp.concatenate([upper, lower], axis=0)

            def product(score, top, weight):
                acc = jnp.dot(with_ones(v_own[there(g)]), weight, preferred_element_type=jnp.float32)
                return acc[:WIDTH], acc[WIDTH : WIDTH + 1], jnp.concatenate(top[3:], axis=1)

            return score, top, weight, product

        done = pipelined([u(g) for g in range(GROUP) for u in (unit_x, unit_z, unit_d)])
        own, mate = [], []
        for g in range(GROUP):
            x, z, d = [done[3 * g + j][3] for j in range(3)]
            own.append(mix(d, [e[:, :rows] for e in x]))
            mate.append(mix(z, [e[:, rows:] for e in x]))
        for g in range(GROUP):
            part[rows_at(i, g)] = own[g][0]
            msg[rows_at(i, g, MSG)] = mate[g][0].astype(jnp.bfloat16)
        part_lse[i] = stack_rows([lse for _, lse in own], 8)
        stat = jnp.concatenate([lse for _, lse in mate], axis=0)
        high = stat.astype(jnp.bfloat16).astype(jnp.float32)
        mid = (stat - high).astype(jnp.bfloat16).astype(jnp.float32)
        stat = stack_rows([high, mid, stat - high - mid, jnp.zeros((1, rows), jnp.float32)], 4)
        msg[pl.ds(pl.multiple_of(i * MSG + STEP, 16), STAT)] = stat.astype(jnp.bfloat16)
        return carry

    lax.fori_loop(0, part_lse.shape[0], one_group, 0)


VMEM = pl.BlockSpec(memory_space=pltpu.VMEM)
ANY = pl.BlockSpec(memory_space=pl.ANY)


def attend(arguments, q_mate, came, first, skip, groups):
    rows = q_mate.shape[1]
    size, heads = groups * STEP, groups * GROUP
    q, k, v = arguments
    return pl.pallas_call(
        lambda *refs: attend_kernel(first, skip, *refs),
        in_specs=[ANY] * 2 + [VMEM] * 6,
        out_specs=[VMEM] * 3,
        out_shape=[
            jax.ShapeDtypeStruct((size, rows), jnp.float32),
            jax.ShapeDtypeStruct((groups, 8, rows), jnp.float32),
            jax.ShapeDtypeStruct((groups * MSG, rows), jnp.bfloat16),
        ],
        scratch_shapes=[pltpu.VMEM((size, rows), jnp.bfloat16)] * 2 + [pltpu.SemaphoreType.DMA((groups, 2))],
        compiler_params=pltpu.CompilerParams(vmem_limit_bytes=12 * 2**20),
        cost_estimate=pl.CostEstimate(
            flops=heads * 4 * 4 * 4 * rows * rows * WIDTH,
            bytes_accessed=heads * WIDTH * rows * 24,
            transcendentals=heads * 4 * rows * rows,
        ),
        name="attend",
    )(q, q_mate, k, v, *came)


def merge_kernel(part, part_lse, msg, *rest):
    out = rest[-1]
    at = 0
    for before in rest[:-1]:
        out[pl.ds(at, before.shape[0])] = before[...]
        at += before.shape[0]
    for i in range(part_lse.shape[0]):
        stat = msg[pl.ds(i * MSG + STEP, STAT)].astype(jnp.float32)
        lse = stat[:GROUP] + stat[GROUP : 2 * GROUP] + stat[2 * GROUP : 3 * GROUP]
        gap = lse - part_lse[i, :GROUP]
        mine, theirs = 1.0 / (1.0 + jnp.exp2(gap)), 1.0 / (1.0 + jnp.exp2(-gap))
        for g in range(GROUP):
            row, src = i * STEP + g * WIDTH, pl.ds(i * MSG + g * WIDTH, WIDTH)
            both = part[pl.ds(row, WIDTH)] * mine[g : g + 1] + msg[src].astype(jnp.float32) * theirs[g : g + 1]
            out[pl.ds(at + row, WIDTH)] = both.astype(jnp.bfloat16)


def merge(part, part_lse, msg, *before):
    size, rows = part.shape
    done = sum(b.shape[0] for b in before)
    return pl.pallas_call(
        merge_kernel,
        in_specs=[VMEM] * (3 + len(before)),
        out_specs=VMEM,
        out_shape=jax.ShapeDtypeStruct((done + size, rows), jnp.bfloat16),
        compiler_params=pltpu.CompilerParams(vmem_limit_bytes=12 * 2**20),
        cost_estimate=pl.CostEstimate(flops=size * rows * 4, bytes_accessed=size * rows * 8, transcendentals=0),
        name="merge",
    )(part, part_lse, msg, *before)


def shards(queries, keys, values):
    length = lax.axis_size("seq")
    position = lax.axis_index("seq")
    column = position % 4
    q, k, v = queries.T, keys.T, values.T
    swap = [(i, i ^ 1) for i in range(length)]
    to_x = [(i, i + (3, 1, 3, -3)[i % 4]) for i in range(length)]
    to_x = [(i, j) for i, j in to_x if j < length]
    to_y = [(i, i + 4) for i in range(length - 4) if i % 2]
    to_y0 = [(i, i + 4) for i in range(length - 4) if i % 4 != 2]

    cut = HALVES[0] * STEP
    k1, k2, v1, v2 = k[:cut], k[cut:], v[:cut], v[cut:]
    r1 = lax.ppermute(k, "seq", to_x)
    y1, y2 = lax.ppermute(v1, "seq", to_y), lax.ppermute(v2, "seq", to_y)
    q_mate = lax.ppermute(q, "seq", swap)
    send = jnp.where(column == 3, y1, v1)
    r3 = lax.ppermute(send, "seq", to_x)
    r1 = lax.optimization_barrier((r1, send))[0]
    send = jnp.where(column == 0, r1[:cut], k1)
    y3 = lax.ppermute(send, "seq", to_y0)
    r1, y2 = lax.optimization_barrier((r1, y2, send))[:2]
    send = jnp.where(column == 0, r1[cut:], k2)
    y4 = lax.ppermute(send, "seq", to_y0)
    r4 = lax.ppermute(jnp.where(column == 3, y2, v2), "seq", to_x)
    halves, arguments = ((r1, r3, y1, y3), (r1, r4, y2, y4)), (q, k, v)
    results, first = [], 0
    for groups in CHUNKS:
        half = int(first >= HALVES[0])
        part, lse, msg = attend(arguments, q_mate, halves[half], first, first - half * HALVES[0], groups)
        q_mate, msg = lax.optimization_barrier((q_mate, msg))
        results.append((part, lse, lax.ppermute(msg, "seq", swap)))
        first += groups
    before = [merge(*result) for result in results[:-1]]
    return merge(*results[-1], *before).T


def solution(mesh):
    return jax.shard_map(
        shards,
        mesh=mesh,
        in_specs=(P(("hist", "seq"), None), P(("hist", "seq"), None), P(("hist", "seq"), None)),
        out_specs=P(("hist", "seq"), None),
        check_vma=False,
    )
```

```python
import jax
import jax.numpy as jnp
from jax import lax
from jax.experimental import pallas as pl
from jax.experimental.pallas import tpu as pltpu
from jax.sharding import PartitionSpec as P

HEADS = 25
WIDTH = 64
GROUP = 5
HALVES = (2, 3)
CHUNKS = (2, 2, 1)
STEP = GROUP * WIDTH
ONES = 16
STAT = 16
MSG = STEP + STAT
SCALE = WIDTH ** -0.5 * 1.4426950408889634
NEG = -1e30


def scores(key_cols, query_cols):
    return lax.dot_general(key_cols, query_cols, (((0,), (0,)), ((), ())), preferred_element_type=jnp.float32)


def fold_max(tile):
    return jnp.max(tile.reshape(tile.shape[0] // 8, 8, tile.shape[1]), axis=0)


def top_of(folded):
    return jnp.max(folded, axis=0, keepdims=True) * SCALE


def with_ones(value):
    return jnp.concatenate([value, jnp.ones((ONES, value.shape[1]), value.dtype)], axis=0)


def weights(score, top):
    return jnp.exp2(score * SCALE - top).astype(jnp.bfloat16)


def pipelined(units):
    results, depth = [[] for _ in units], len(units[0])
    for i in range(len(units) + depth - 1):
        for stage in range(depth):
            if 0 <= i - stage < len(units):
                done = results[i - stage]
                done.append(units[i - stage][stage](*done))
    return results


def stack_rows(rows, size):
    fill = [jnp.zeros_like(rows[0])] * (size - len(rows))
    return jnp.concatenate(list(rows) + fill, axis=0)


def mix(a, b):
    (acc_a, total_a, top_a), (acc_b, total_b, top_b) = a, b
    top = jnp.maximum(top_a, top_b)
    factor_a, factor_b = jnp.exp2(top_a - top), jnp.exp2(top_b - top)
    total = total_a * factor_a + total_b * factor_b
    return acc_a * (factor_a / total) + acc_b * (factor_b / total), top + jnp.log2(total)


def attend_kernel(first, skip, q_own, q_mate, k_own, v_own, r1, r3, y1, y3, part, part_lse, msg):
    position = lax.axis_index("seq")
    even, is0 = position % 2 == 0, position % 4 == 0
    ok_x, ok_z = (position >= 3) | (even & (position >= 1)), even | (position >= 4)
    rows = q_own.shape[1]
    half = rows // 2
    later = lax.broadcasted_iota(jnp.int32, (half, half), 0) > lax.broadcasted_iota(jnp.int32, (half, half), 1)

    def one_group(i, carry):
        def rows_at(group, g, step=STEP):
            return pl.ds(pl.multiple_of(group * step + g * WIDTH, 16), WIDTH)

        def here(g):
            return rows_at(skip + i, g)

        def there(g):
            return rows_at(first + i, g)

        def unit(score, value, ok):
            def top(s):
                return top_of(fold_max(s))

            def weight(s, top):
                return weights(s, top)

            def product(s, top, weight):
                acc = jnp.dot(with_ones(value()), weight, preferred_element_type=jnp.float32)
                return acc[:WIDTH], acc[WIDTH : WIDTH + 1], jnp.where(ok, top, NEG)

            return score, top, weight, product

        def unit_x(g):
            def score():
                key = jnp.where(is0, r3[here(g)], r1[here(g)])
                return scores(key, jnp.concatenate([q_own[there(g)], q_mate[there(g)]], axis=1))

            return unit(score, lambda: jnp.where(is0, y3[here(g)], r3[here(g)]), ok_x)

        def unit_z(g):
            def score():
                return scores(jnp.where(even, k_own[there(g)], y1[here(g)]), q_mate[there(g)])

            return unit(score, lambda: jnp.where(even, v_own[there(g)], y3[here(g)]), ok_z)

        def unit_d(g):
            def score():
                q, k = q_own[there(g)], k_own[there(g)]
                return scores(k[:, :half], q), scores(k[:, half:], q[:, half:])

            def top(score):
                first, last = score
                corner, last = jnp.where(later, NEG, first[:, :half]), jnp.where(later, NEG, last)
                right = first[:, half:]
                top_a, top_b = top_of(fold_max(corner)), top_of(jnp.maximum(fold_max(right), fold_max(last)))
                return corner, right, last, top_a, top_b

            def weight(score, top):
                corner, right, last, top_a, top_b = top
                upper = jnp.concatenate([weights(corner, top_a), weights(right, top_b)], axis=1)
                lower = jnp.concatenate([jnp.zeros((half, half), jnp.bfloat16), weights(last, top_b)], axis=1)
                return jnp.concatenate([upper, lower], axis=0)

            def product(score, top, weight):
                acc = jnp.dot(with_ones(v_own[there(g)]), weight, preferred_element_type=jnp.float32)
                return acc[:WIDTH], acc[WIDTH : WIDTH + 1], jnp.concatenate(top[3:], axis=1)

            return score, top, weight, product

        done = pipelined([u(g) for g in range(GROUP) for u in (unit_x, unit_z, unit_d)])
        own, mate = [], []
        for g in range(GROUP):
            x, z, d = [done[3 * g + j][3] for j in range(3)]
            own.append(mix(d, [e[:, :rows] for e in x]))
            mate.append(mix(z, [e[:, rows:] for e in x]))
        for g in range(GROUP):
            part[rows_at(i, g)] = own[g][0]
            msg[rows_at(i, g, MSG)] = mate[g][0].astype(jnp.bfloat16)
        part_lse[i] = stack_rows([lse for _, lse in own], 8)
        stat = jnp.concatenate([lse for _, lse in mate], axis=0)
        high = stat.astype(jnp.bfloat16).astype(jnp.float32)
        mid = (stat - high).astype(jnp.bfloat16).astype(jnp.float32)
        stat = stack_rows([high, mid, stat - high - mid, jnp.zeros((1, rows), jnp.float32)], 4)
        msg[pl.ds(pl.multiple_of(i * MSG + STEP, 16), STAT)] = stat.astype(jnp.bfloat16)
        return carry

    lax.fori_loop(0, part_lse.shape[0], one_group, 0)


VMEM = pl.BlockSpec(memory_space=pltpu.VMEM)


def attend(arguments, q_mate, came, first, skip, groups):
    rows = q_mate.shape[1]
    size, heads = groups * STEP, groups * GROUP
    q, k, v = arguments
    return pl.pallas_call(
        lambda *refs: attend_kernel(first, skip, *refs),
        in_specs=[VMEM] * 8,
        out_specs=[VMEM] * 3,
        out_shape=[
            jax.ShapeDtypeStruct((size, rows), jnp.float32),
            jax.ShapeDtypeStruct((groups, 8, rows), jnp.float32),
            jax.ShapeDtypeStruct((groups * MSG, rows), jnp.bfloat16),
        ],
        compiler_params=pltpu.CompilerParams(vmem_limit_bytes=24 * 2**20),
        cost_estimate=pl.CostEstimate(
            flops=heads * 4 * 4 * 4 * rows * rows * WIDTH,
            bytes_accessed=heads * WIDTH * rows * 24,
            transcendentals=heads * 4 * rows * rows,
        ),
        name="attend",
    )(q, q_mate, k, v, *came)


def merge_kernel(part, part_lse, msg, *rest):
    out = rest[-1]
    at = 0
    for before in rest[:-1]:
        out[pl.ds(at, before.shape[0])] = before[...]
        at += before.shape[0]
    for i in range(part_lse.shape[0]):
        stat = msg[pl.ds(i * MSG + STEP, STAT)].astype(jnp.float32)
        lse = stat[:GROUP] + stat[GROUP : 2 * GROUP] + stat[2 * GROUP : 3 * GROUP]
        gap = lse - part_lse[i, :GROUP]
        mine, theirs = 1.0 / (1.0 + jnp.exp2(gap)), 1.0 / (1.0 + jnp.exp2(-gap))
        for g in range(GROUP):
            row, src = i * STEP + g * WIDTH, pl.ds(i * MSG + g * WIDTH, WIDTH)
            both = part[pl.ds(row, WIDTH)] * mine[g : g + 1] + msg[src].astype(jnp.float32) * theirs[g : g + 1]
            out[pl.ds(at + row, WIDTH)] = both.astype(jnp.bfloat16)


def merge(part, part_lse, msg, *before):
    size, rows = part.shape
    done = sum(b.shape[0] for b in before)
    return pl.pallas_call(
        merge_kernel,
        in_specs=[VMEM] * (3 + len(before)),
        out_specs=VMEM,
        out_shape=jax.ShapeDtypeStruct((done + size, rows), jnp.bfloat16),
        compiler_params=pltpu.CompilerParams(vmem_limit_bytes=24 * 2**20),
        cost_estimate=pl.CostEstimate(flops=size * rows * 4, bytes_accessed=size * rows * 8, transcendentals=0),
        name="merge",
    )(part, part_lse, msg, *before)


def shards(queries, keys, values):
    length = lax.axis_size("seq")
    position = lax.axis_index("seq")
    column = position % 4
    q, k, v = queries.T, keys.T, values.T
    swap = [(i, i ^ 1) for i in range(length)]
    to_x = [(i, i + (3, 1, 3, -3)[i % 4]) for i in range(length)]
    to_x = [(i, j) for i, j in to_x if j < length]
    to_y = [(i, i + 4) for i in range(length - 4) if i % 2]
    to_y0 = [(i, i + 4) for i in range(length - 4) if i % 4 != 2]

    cut = HALVES[0] * STEP
    k1, k2, v1, v2 = k[:cut], k[cut:], v[:cut], v[cut:]

    r1, y1 = lax.ppermute(jnp.where(column == 3, v1, k1), "seq", to_x), lax.ppermute(k1, "seq", to_y)
    r2, y2 = lax.ppermute(jnp.where(column == 3, v2, k2), "seq", to_x), lax.ppermute(k2, "seq", to_y)
    q_mate = lax.ppermute(q, "seq", swap)
    to_send = jnp.where(column == 3, y1, v1), jnp.where(column == 0, r1, v1)
    y1, r1 = lax.optimization_barrier((y1, r1))
    r3, y3 = lax.ppermute(to_send[0], "seq", to_x), lax.ppermute(to_send[1], "seq", to_y0)
    r2, y2 = lax.optimization_barrier((r2, y2, *to_send))[:2]
    to_send = jnp.where(column == 3, y2, v2), jnp.where(column == 0, r2, v2)
    r4, y4 = lax.ppermute(to_send[0], "seq", to_x), lax.ppermute(to_send[1], "seq", to_y0)
    halves, arguments = ((r1, r3, y1, y3), (r2, r4, y2, y4)), (q, k, v)
    results, first = [], 0
    for groups in CHUNKS:
        half = int(first >= HALVES[0])
        part, lse, msg = attend(arguments, q_mate, halves[half], first, first - half * HALVES[0], groups)
        q_mate, msg = lax.optimization_barrier((q_mate, msg))
        results.append((part, lse, lax.ppermute(msg, "seq", swap)))
        first += groups
    before = [merge(*result) for result in results[:-1]]
    return merge(*results[-1], *before).T


def solution(mesh):
    return jax.shard_map(
        shards,
        mesh=mesh,
        in_specs=(P(("hist", "seq"), None), P(("hist", "seq"), None), P(("hist", "seq"), None)),
        out_specs=P(("hist", "seq"), None),
        check_vma=False,
    )
```

```python
import jax
import jax.numpy as jnp
from jax import lax
from jax.experimental import pallas as pl
from jax.experimental.pallas import tpu as pltpu
from jax.sharding import PartitionSpec as P

HEADS = 25
WIDTH = 64
GROUP = 5
HALVES = (2, 3)
CHUNKS = (2, 2, 1)
STEP = GROUP * WIDTH
ONES = 16
STAT = 16
MSG = STEP + STAT
SCALE = WIDTH ** -0.5 * 1.4426950408889634
NEG = -1e30


def scores(key_cols, query_cols):
    return lax.dot_general(key_cols, query_cols, (((0,), (0,)), ((), ())), preferred_element_type=jnp.float32)


def fold_max(tile):
    return jnp.max(tile.reshape(tile.shape[0] // 8, 8, tile.shape[1]), axis=0)


def top_of(folded):
    return jnp.max(folded, axis=0, keepdims=True) * SCALE


def with_ones(value):
    return jnp.concatenate([value, jnp.ones((ONES, value.shape[1]), value.dtype)], axis=0)


def weights(score, top):
    return jnp.exp2(score * SCALE - top).astype(jnp.bfloat16)


def pipelined(units):
    results, depth = [[] for _ in units], len(units[0])
    for i in range(len(units) + depth - 1):
        for stage in range(depth):
            if 0 <= i - stage < len(units):
                done = results[i - stage]
                done.append(units[i - stage][stage](*done))
    return results


def stack_rows(rows, size):
    fill = [jnp.zeros_like(rows[0])] * (size - len(rows))
    return jnp.concatenate(list(rows) + fill, axis=0)


def mix(a, b):
    (acc_a, total_a, top_a), (acc_b, total_b, top_b) = a, b
    top = jnp.maximum(top_a, top_b)
    factor_a, factor_b = jnp.exp2(top_a - top), jnp.exp2(top_b - top)
    total = total_a * factor_a + total_b * factor_b
    return acc_a * (factor_a / total) + acc_b * (factor_b / total), top + jnp.log2(total)


def attend_kernel(for_mate, first, skip, query, k_own, v_own, r1, r3, y1, y3, out, *out_lse):
    position = lax.axis_index("seq")
    even, is0 = position % 2 == 0, position % 4 == 0
    ok_x, ok_z = (position >= 3) | (even & (position >= 1)), even | (position >= 4)
    rows = query.shape[1]
    half = rows // 2
    later = lax.broadcasted_iota(jnp.int32, (half, half), 0) > lax.broadcasted_iota(jnp.int32, (half, half), 1)

    def one_group(i, carry):
        def rows_at(group, g, step=STEP):
            return pl.ds(pl.multiple_of(group * step + g * WIDTH, 16), WIDTH)

        def here(g):
            return rows_at(skip + i, g)

        def there(g):
            return rows_at(first + i, g)

        def unit(score, value, ok):
            def top(s):
                return top_of(fold_max(s))

            def weight(s, top):
                return weights(s, top)

            def product(s, top, weight):
                acc = jnp.dot(with_ones(value()), weight, preferred_element_type=jnp.float32)
                return acc[:WIDTH], acc[WIDTH : WIDTH + 1], jnp.where(ok, top, NEG)

            return score, top, weight, product

        def unit_x(g):
            def score():
                key = jnp.where(is0, r3[here(g)], r1[here(g)])
                return scores(key, query[there(g)])

            return unit(score, lambda: jnp.where(is0, y3[here(g)], r3[here(g)]), ok_x)

        def unit_z(g):
            def score():
                return scores(jnp.where(even, k_own[there(g)], y1[here(g)]), query[there(g)])

            return unit(score, lambda: jnp.where(even, v_own[there(g)], y3[here(g)]), ok_z)

        def unit_d(g):
            def score():
                q, k = query[there(g)], k_own[there(g)]
                return scores(k[:, :half], q), scores(k[:, half:], q[:, half:])

            def top(score):
                first, last = score
                corner, last = jnp.where(later, NEG, first[:, :half]), jnp.where(later, NEG, last)
                right = first[:, half:]
                top_a, top_b = top_of(fold_max(corner)), top_of(jnp.maximum(fold_max(right), fold_max(last)))
                return corner, right, last, top_a, top_b

            def weight(score, top):
                corner, right, last, top_a, top_b = top
                upper = jnp.concatenate([weights(corner, top_a), weights(right, top_b)], axis=1)
                lower = jnp.concatenate([jnp.zeros((half, half), jnp.bfloat16), weights(last, top_b)], axis=1)
                return jnp.concatenate([upper, lower], axis=0)

            def product(score, top, weight):
                acc = jnp.dot(with_ones(v_own[there(g)]), weight, preferred_element_type=jnp.float32)
                return acc[:WIDTH], acc[WIDTH : WIDTH + 1], jnp.concatenate(top[3:], axis=1)

            return score, top, weight, product

        done = pipelined([u(g) for g in range(GROUP) for u in (unit_x, unit_z if for_mate else unit_d)])
        mixed = [mix(done[2 * g + 1][3], done[2 * g][3]) for g in range(GROUP)]
        if not for_mate:
            for g in range(GROUP):
                out[rows_at(i, g)] = mixed[g][0]
            out_lse[0][i] = stack_rows([lse for _, lse in mixed], 8)
            return carry
        for g in range(GROUP):
            out[rows_at(i, g, MSG)] = mixed[g][0].astype(jnp.bfloat16)
        stat = jnp.concatenate([lse for _, lse in mixed], axis=0)
        high = stat.astype(jnp.bfloat16).astype(jnp.float32)
        mid = (stat - high).astype(jnp.bfloat16).astype(jnp.float32)
        stat = stack_rows([high, mid, stat - high - mid, jnp.zeros((1, rows), jnp.float32)], 4)
        out[pl.ds(pl.multiple_of(i * MSG + STEP, 16), STAT)] = stat.astype(jnp.bfloat16)
        return carry

    lax.fori_loop(0, out.shape[0] // (MSG if for_mate else STEP), one_group, 0)


VMEM = pl.BlockSpec(memory_space=pltpu.VMEM)


def attend(for_mate, query, k, v, came, first, skip, groups):
    rows = query.shape[1]
    size, heads = groups * STEP, groups * GROUP
    shapes = [
        jax.ShapeDtypeStruct((size, rows), jnp.float32),
        jax.ShapeDtypeStruct((groups, 8, rows), jnp.float32),
    ]
    if for_mate:
        shapes = [jax.ShapeDtypeStruct((groups * MSG, rows), jnp.bfloat16)]
    return pl.pallas_call(
        lambda *refs: attend_kernel(for_mate, first, skip, *refs),
        in_specs=[VMEM] * 7,
        out_specs=[VMEM] * len(shapes),
        out_shape=shapes,
        compiler_params=pltpu.CompilerParams(vmem_limit_bytes=24 * 2**20),
        cost_estimate=pl.CostEstimate(
            flops=heads * 6 * 2 * 4 * rows * rows * WIDTH,
            bytes_accessed=heads * WIDTH * rows * 12,
            transcendentals=heads * 2 * rows * rows,
        ),
        name="mate" if for_mate else "own",
    )(query, k, v, *came)


def merge_kernel(part, part_lse, msg, *rest):
    out = rest[-1]
    at = 0
    for before in rest[:-1]:
        out[pl.ds(at, before.shape[0])] = before[...]
        at += before.shape[0]
    for i in range(part_lse.shape[0]):
        stat = msg[pl.ds(i * MSG + STEP, STAT)].astype(jnp.float32)
        lse = stat[:GROUP] + stat[GROUP : 2 * GROUP] + stat[2 * GROUP : 3 * GROUP]
        gap = lse - part_lse[i, :GROUP]
        mine, theirs = 1.0 / (1.0 + jnp.exp2(gap)), 1.0 / (1.0 + jnp.exp2(-gap))
        for g in range(GROUP):
            row, src = i * STEP + g * WIDTH, pl.ds(i * MSG + g * WIDTH, WIDTH)
            both = part[pl.ds(row, WIDTH)] * mine[g : g + 1] + msg[src].astype(jnp.float32) * theirs[g : g + 1]
            out[pl.ds(at + row, WIDTH)] = both.astype(jnp.bfloat16)


def merge(part, part_lse, msg, *before):
    size, rows = part.shape
    done = sum(b.shape[0] for b in before)
    return pl.pallas_call(
        merge_kernel,
        in_specs=[VMEM] * (3 + len(before)),
        out_specs=VMEM,
        out_shape=jax.ShapeDtypeStruct((done + size, rows), jnp.bfloat16),
        compiler_params=pltpu.CompilerParams(vmem_limit_bytes=24 * 2**20),
        cost_estimate=pl.CostEstimate(flops=size * rows * 4, bytes_accessed=size * rows * 8, transcendentals=0),
        name="merge",
    )(part, part_lse, msg, *before)


def shards(queries, keys, values):
    length = lax.axis_size("seq")
    position = lax.axis_index("seq")
    column = position % 4
    q, k, v = queries.T, keys.T, values.T
    swap = [(i, i ^ 1) for i in range(length)]
    to_x = [(i, i + (3, 1, 3, -3)[i % 4]) for i in range(length)]
    to_x = [(i, j) for i, j in to_x if j < length]
    to_y = [(i, i + 4) for i in range(length - 4) if i % 2]
    to_y0 = [(i, i + 4) for i in range(length - 4) if i % 4 != 2]

    cut = HALVES[0] * STEP
    k1, k2, v1, v2 = k[:cut], k[cut:], v[:cut], v[cut:]

    r1, y1 = lax.ppermute(jnp.where(column == 3, v1, k1), "seq", to_x), lax.ppermute(k1, "seq", to_y)
    r2, y2 = lax.ppermute(jnp.where(column == 3, v2, k2), "seq", to_x), lax.ppermute(k2, "seq", to_y)
    q_mate = lax.ppermute(q, "seq", swap)
    to_send = jnp.where(column == 3, y1, v1), jnp.where(column == 0, r1, v1)
    y1, r1 = lax.optimization_barrier((y1, r1))
    r3, y3 = lax.ppermute(to_send[0], "seq", to_x), lax.ppermute(to_send[1], "seq", to_y0)
    r2, y2 = lax.optimization_barrier((r2, y2, *to_send))[:2]
    to_send = jnp.where(column == 3, y2, v2), jnp.where(column == 0, r2, v2)
    r4, y4 = lax.ppermute(to_send[0], "seq", to_x), lax.ppermute(to_send[1], "seq", to_y0)
    halves = (r1, r3, y1, y3), (r2, r4, y2, y4)
    results, first = [], 0
    for groups in CHUNKS:
        half = int(first >= HALVES[0])
        place = halves[half], first, first - half * HALVES[0], groups
        (msg,) = attend(True, q_mate, k, v, *place)
        q_mate, q, msg = lax.optimization_barrier((q_mate, q, msg))
        results.append((*attend(False, q, k, v, *place), lax.ppermute(msg, "seq", swap)))
        first += groups
    before = [merge(*result) for result in results[:-1]]
    return merge(*results[-1], *before).T


def solution(mesh):
    return jax.shard_map(
        shards,
        mesh=mesh,
        in_specs=(P(("hist", "seq"), None), P(("hist", "seq"), None), P(("hist", "seq"), None)),
        out_specs=P(("hist", "seq"), None),
        check_vma=False,
    )
```
